256 devices in a mesh: row: 8 (over z), col: 16 (over x_hi, y, core), slab: 2 (over x_lo).
Axes of the slice: x: 4 (x_hi: 2, x_lo: 2; x = x_hi * 2 + x_lo), y: 4, z: 8, core: 2. Of those that a mesh axis runs over, the one named last changes fastest.
Arguments:
- amplitudes: bfloat16 [2, 8192, 2048], P('slab', 'row', 'col'), may hold values from -6 to 6
- integrals: bfloat16 [2048, 24576], P(('row', 'slab'), 'col'), may hold values from -0.125 to 0.125
- pair_count: int32 [2], replicated, may hold values from 4096 to 8192, as said below
- pair_sym: int32 [2, 64], P('slab', 'row'), may hold values from 0 to 1, as said below
- vir_sym: int32 [16], replicated, may hold values from 0 to 1
- out_sym: int32 [192], P('col'), may hold values from 0 to 1, as said below
Outputs:
- ladder: bfloat16 [2, 8192, 24576], P('slab', 'row', 'col')
The draws below stay inside these ranges and needn't reach their ends.
Inputs may be any that keep to these rules, and one draw needn't show every extreme that they name: `pair_count`: one slab has all 8192 pairs live. `pair_sym`: in each slab, of the 8 row tiles j * 8 to j * 8 + 8 - 1 (those of one device), exactly half have block id 0 and half block id 1. `out_sym`: of the 12 output tiles j * 12 to j * 12 + 12 - 1 (those of one device), exactly half have block id 0 and half block id 1.
All inputs are finite; a program needn't handle non-finite values.
Results may differ from the reference program's by a relative error of at most 0.003.
Values may be sent and summed in bfloat16 or wider, within the bound.
No kernel may reach another device: no remote copies, remote signals or barrier semaphores. Data moves between devices by JAX's collectives and lax.ppermute only.
A program may use at most 64 MiB of HBM per device.

```python
import jax
import jax.numpy as jnp

TILE = 128
MT = 8
NT = 12
K_TILES = 16
KSUM = 2048
MS = 8192
NOUT = 24576
N_SLAB = 2


def balanced_ids(key, blocks, per_block):
    base = (jnp.arange(per_block, dtype=jnp.int32) >= per_block // 2).astype(jnp.int32)
    block_keys = jax.random.split(key, blocks)

    def shuffle_block(block_key):
        return jax.random.permutation(block_key, base)
    return jax.vmap(shuffle_block)(block_keys)


def draw_pair_count(key, part):
    key = jax.random.fold_in(key, 7)
    first_key, second_key = jax.random.split(key)
    full_slab = jax.random.randint(first_key, (), 0, N_SLAB)
    others = jax.random.randint(second_key, (N_SLAB,), MS // 2, MS + 1)
    return jnp.where(jnp.arange(N_SLAB) == full_slab, MS, others).astype(jnp.int32)


def draw_pair_sym(key, part):
    key = jax.random.fold_in(key, 11)
    groups = MS // (MT * TILE)
    return balanced_ids(key, N_SLAB * groups, MT).reshape(N_SLAB, MS // TILE).astype(jnp.int32)


def draw_out_sym(key, part):
    key = jax.random.fold_in(key, 13)
    groups = NOUT // (NT * TILE)
    return balanced_ids(key, groups, NT).reshape(NOUT // TILE).astype(jnp.int32)


def plant(result, key, smallest, largest):
    dims = result.shape
    spot = [jax.random.randint(jax.random.fold_in(key, axis), (), 0, dims[axis]) for axis in range(len(dims))]
    result = result.at[tuple(spot)].set(smallest)
    longest = dims.index(max(dims))
    spot[longest] = (spot[longest] + 1) % dims[longest]
    return result.at[tuple(spot)].set(largest)


def block_levels(stream_key, extent, shards, low, high):
    def one(dim, blocks):
        draws = jax.random.uniform(jax.random.fold_in(jax.random.fold_in(stream_key, 6), dim), (blocks,), jnp.float32, low / len(shards), high / len(shards))
        return jnp.repeat(jnp.exp(draws), extent[dim] // blocks).reshape((-1,) + (1,) * (len(extent) - dim - 1))

    level = one(*shards[0])
    for cut in shards[1:]:
        level = level * one(*cut)
    return level


def noise(own_key, shape, spread, limit, pieces=(), kind=jnp.bfloat16):
    drawn = spread * jax.random.normal(own_key, shape, jnp.float32)
    if pieces:
        drawn = drawn * block_levels(own_key, shape, pieces, -0.22, 0.18)
    return jnp.clip(drawn, -limit, limit).astype(kind)


def setup_inputs(seed: int = 0) -> dict:
    key_of = jax.random.split(jax.random.key(seed), 7)
    return {
        "amplitudes": noise(key_of[0], (N_SLAB, MS, KSUM), 1.0, 6.0, ((0, 2), (1, 8), (2, 16))),
        "integrals": noise(key_of[1], (KSUM, NOUT), KSUM ** -0.5, 0.125, ((0, 16), (1, 16))),
        "pair_count": draw_pair_count(jax.random.fold_in(key_of[6], 71), 0),
        "pair_sym": draw_pair_sym(jax.random.fold_in(key_of[6], 71), 0),
        "vir_sym": plant(jax.random.randint(key_of[4], (K_TILES,), 0, 2), jax.random.fold_in(key_of[4], 1), 0, 1).astype(jnp.int32),
        "out_sym": draw_out_sym(jax.random.fold_in(key_of[6], 71), 0),
    }


def reference(amplitudes, integrals, pair_count, pair_sym, vir_sym, out_sym):
    zero = jnp.zeros((), jnp.bfloat16)
    vir_cols = jnp.repeat(vir_sym, TILE)
    out_cols = jnp.repeat(out_sym, TILE)
    ints_kept = jnp.where(vir_cols[:, None] == out_cols[None, :], integrals, zero)
    results = []
    for slab_index in range(N_SLAB):
        pair_rows = jnp.repeat(pair_sym[slab_index], TILE)
        amps_kept = jnp.where(pair_rows[:, None] == vir_cols[None, :], amplitudes[slab_index], zero)
        product = jnp.dot(amps_kept, ints_kept, preferred_element_type=jnp.float32)
        live = jnp.arange(MS, dtype=jnp.int32) < pair_count[slab_index]
        results.append(jnp.where(live[:, None], product, 0.0).astype(jnp.bfloat16))
    return jnp.stack(results)
```

```python
import functools

import jax
import jax.numpy as jnp
from jax import lax
from jax.experimental import pallas as pl
from jax.experimental.pallas import tpu as pltpu
from jax.sharding import PartitionSpec as P

TILE = 128
VMEM_LIMIT = 48 * 1024 * 1024


def pack_kernel(pair_tiles, vir, out_tiles, amp, ints, amp_out, int_out):
    amp_id = vir[lax.axis_index("col")]
    int_id = vir[lax.axis_index("row") * lax.axis_size("slab") + lax.axis_index("slab")]
    count = jnp.int32(0)
    for tile in range(pair_tiles.shape[1]):
        match = pair_tiles[0, tile] == amp_id

        @pl.when(match)
        def _():
            start = pl.multiple_of(count * TILE, TILE)
            amp_out[pl.ds(start, TILE), :] = amp[0, tile * TILE : (tile + 1) * TILE, :]

        count = count + match.astype(jnp.int32)
    count = jnp.int32(0)
    for tile in range(out_tiles.shape[0]):
        match = out_tiles[tile] == int_id

        @pl.when(match)
        def _():
            start = pl.multiple_of(count * TILE, TILE)
            int_out[:, pl.ds(start, TILE)] = ints[:, tile * TILE : (tile + 1) * TILE]

        count = count + match.astype(jnp.int32)


def pack(amplitudes, integrals, pair_sym, vir_sym, out_sym):
    smem = pl.BlockSpec(memory_space=pltpu.SMEM)
    vmem = pl.BlockSpec(memory_space=pltpu.VMEM)
    rows, width = amplitudes.shape[1:]
    depth, cols = integrals.shape
    return pl.pallas_call(
        pack_kernel,
        out_shape=(
            jax.ShapeDtypeStruct((rows // 2, width), jnp.bfloat16),
            jax.ShapeDtypeStruct((depth, cols // 2), jnp.bfloat16),
        ),
        in_specs=[smem, smem, smem, vmem, vmem],
        out_specs=(vmem, vmem),
    )(pair_sym, vir_sym, out_sym, amplitudes, integrals)


def ladder_kernel(pairs, k_tiles, rows, cols, *refs):
    pair_count, pair_tiles, vir, out_tiles, amp_own, amp_other = refs[:6]
    blocks = refs[6 : 6 + k_tiles]
    out = refs[6 + k_tiles]
    amp_buf, int_buf, acc, out_buf, where_k, row_at, col_at, amp_sem, int_sem, out_sem = refs[7 + k_tiles :]
    mt, nt = pair_tiles.shape[1], out_tiles.shape[0]
    col_now, row_now, slab_now = (lax.axis_index(name) for name in ("col", "row", "slab"))
    n_slab, n_row = lax.axis_size("slab"), lax.axis_size("row")

    ones = jnp.int32(0)
    for k in range(k_tiles):
        ones = ones + vir[k]
    zeros = k_tiles - ones
    zero_chunks = (zeros + 1) // 2
    one_chunks = (ones + 1) // 2
    chunks = zero_chunks + one_chunks
    nzero, none = jnp.int32(0), jnp.int32(0)
    for k in range(k_tiles):
        is_one = vir[k]
        where_k[k] = jnp.where(is_one == 1, 2 * zero_chunks + none, nzero)
        none = none + is_one
        nzero = nzero + 1 - is_one

    half = k_tiles // 2
    copies = []
    for core in range(2):
        source = amp_own if core == 0 else amp_other
        for j in range(half):
            y, hi = j // 2, j % 2
            k = (hi * (half // 2) + y) * 2 + jnp.bitwise_xor(col_now % 2, core)
            copies.append(
                pltpu.make_async_copy(
                    source.at[pl.ds(j * (rows // 2), rows // 2)],
                    amp_buf.at[where_k[k]],
                    amp_sem.at[core * half + j],
                )
            )
    for index, (step, other) in enumerate(pairs):
        k = lax.rem(row_now + step + n_row, n_row) * n_slab + (slab_now if other == 0 else 1 - slab_now)
        copies.append(pltpu.make_async_copy(blocks[index], int_buf.at[where_k[k]], int_sem.at[index]))
    for copy in copies:
        copy.start()

    @pl.when(zeros % 2 == 1)
    def _():
        amp_buf[zeros] = jnp.zeros(amp_buf.shape[1:], amp_buf.dtype)
        int_buf[zeros] = jnp.zeros(int_buf.shape[1:], int_buf.dtype)

    @pl.when(ones % 2 == 1)
    def _():
        last = 2 * zero_chunks + ones
        amp_buf[last] = jnp.zeros(amp_buf.shape[1:], amp_buf.dtype)
        int_buf[last] = jnp.zeros(int_buf.shape[1:], int_buf.dtype)

    out_buf[...] = jnp.zeros(out_buf.shape, out_buf.dtype)
    nzero, none = jnp.int32(0), jnp.int32(0)
    for tile in range(mt):
        is_one = pair_tiles[0, tile]
        row_at[jnp.where(is_one == 1, mt // 2 + none, nzero)] = tile
        none = none + is_one
        nzero = nzero + 1 - is_one
    nzero, none = jnp.int32(0), jnp.int32(0)
    for tile in range(nt):
        is_one = out_tiles[tile]
        col_at[jnp.where(is_one == 1, nt // 2 + none, nzero)] = tile
        none = none + is_one
        nzero = nzero + 1 - is_one

    for copy in copies:
        copy.wait()

    live = pair_count[slab_now] - row_now * rows
    for group in range(2):
        acc[...] = jnp.zeros(acc.shape, acc.dtype)
        first = 0 if group == 0 else zero_chunks
        last = zero_chunks if group == 0 else chunks

        @pl.loop(first, last)
        def _(chunk):
            left = jnp.concatenate([amp_buf[2 * chunk], amp_buf[2 * chunk + 1]], axis=1)
            right = jnp.concatenate([int_buf[2 * chunk], int_buf[2 * chunk + 1]], axis=0)
            acc[...] += jnp.dot(left, right, preferred_element_type=jnp.float32)

        for r in range(mt // 2):
            tile = row_at[group * (mt // 2) + r]
            row_start = pl.multiple_of(tile * TILE, TILE)
            keep = row_start + lax.broadcasted_iota(jnp.int32, (TILE, TILE), 0) < live
            for c in range(nt // 2):
                col_start = pl.multiple_of(col_at[group * (nt // 2) + c] * TILE, TILE)
                value = acc[r * TILE : (r + 1) * TILE, c * TILE : (c + 1) * TILE]
                out_buf[pl.ds(row_start, TILE), pl.ds(col_start, TILE)] = jnp.where(keep, value, 0.0).astype(jnp.bfloat16)
            pltpu.make_async_copy(
                out_buf.at[pl.ds(row_start, TILE)],
                out.at[0, pl.ds(row_start, TILE)],
                out_sem.at[group * (mt // 2) + r],
            ).start()
    for index in range(mt):
        row_start = pl.multiple_of(row_at[index] * TILE, TILE)
        pltpu.make_async_copy(
            out_buf.at[pl.ds(row_start, TILE)], out.at[0, pl.ds(row_start, TILE)], out_sem.at[index]
        ).wait()


def ladder(rows, cols, pairs, pair_count, pair_sym, vir_sym, out_sym, amp_own, amp_other, blocks):
    k_tiles = len(blocks)
    smem = pl.BlockSpec(memory_space=pltpu.SMEM)
    any_space = pl.BlockSpec(memory_space=pl.ANY)
    mt, nt = rows // TILE, cols // TILE
    return pl.pallas_call(
        functools.partial(ladder_kernel, pairs, k_tiles, rows, cols),
        out_shape=jax.ShapeDtypeStruct((1, rows, cols), jnp.bfloat16),
        in_specs=[smem] * 4 + [any_space] * (2 + k_tiles),
        out_specs=any_space,
        scratch_shapes=[
            pltpu.VMEM((k_tiles + 2, rows // 2, TILE), jnp.bfloat16),
            pltpu.VMEM((k_tiles + 2, TILE, cols // 2), jnp.bfloat16),
            pltpu.VMEM((rows // 2, cols // 2), jnp.float32),
            pltpu.VMEM((rows, cols), jnp.bfloat16),
            pltpu.SMEM((k_tiles,), jnp.int32),
            pltpu.SMEM((mt,), jnp.int32),
            pltpu.SMEM((nt,), jnp.int32),
            pltpu.SemaphoreType.DMA((k_tiles,)),
            pltpu.SemaphoreType.DMA((k_tiles,)),
            pltpu.SemaphoreType.DMA((mt,)),
        ],
        compiler_params=pltpu.CompilerParams(vmem_limit_bytes=VMEM_LIMIT),
    )(pair_count, pair_sym, vir_sym, out_sym, amp_own, amp_other, *blocks)


def body(amplitudes, integrals, pair_count, pair_sym, vir_sym, out_sym):
    rows, cols = amplitudes.shape[1], integrals.shape[1]
    n_row, n_col = lax.axis_size("row"), lax.axis_size("col")
    amp, block = pack(amplitudes, integrals, pair_sym, vir_sym, out_sym)

    half = n_col // 2
    across = [[c, c + half] for c in range(half)]
    round_y = [[h * half + y * 2 + core for y in range(half // 2)] for h in range(2) for core in range(2)]
    amp = lax.all_gather(amp, "col", axis=0, tiled=True, axis_index_groups=across)
    amp = lax.all_gather(amp, "col", axis=0, tiled=True, axis_index_groups=round_y)
    amp_other = lax.ppermute(amp, "col", [(c, c ^ 1) for c in range(n_col)])

    up = [(i, (i + 1) % n_row) for i in range(n_row)]
    down = [(i, (i - 1) % n_row) for i in range(n_row)]
    other = lax.ppermute(block, "slab", [(0, 1), (1, 0)])
    blocks = {(0, 0): block, (0, 1): other}
    for step in range(1, n_row // 2 + 1):
        for slab in range(2):
            if step < n_row // 2 or slab == 0:
                blocks[(-step, slab)] = lax.ppermute(blocks[(1 - step, slab)], "row", up)
            if step < n_row // 2 or slab == 1:
                blocks[(step, slab)] = lax.ppermute(blocks[(step - 1, slab)], "row", down)
    pairs = tuple(blocks)
    return ladder(
        rows, cols, pairs, pair_count, pair_sym, vir_sym, out_sym, amp, amp_other, [blocks[p] for p in pairs]
    )


def solution(mesh):
    in_specs = (
        P("slab", "row", "col"),
        P(("row", "slab"), "col"),
        P(),
        P("slab", "row"),
        P(),
        P("col"),
    )
    out_specs = P("slab", "row", "col")
    return jax.shard_map(body, mesh=mesh, in_specs=in_specs, out_specs=out_specs, check_vma=False)
```

```python
import functools

import jax
import jax.numpy as jnp
from jax import lax
from jax.experimental import pallas as pl
from jax.experimental.pallas import tpu as pltpu
from jax.sharding import PartitionSpec as P

TILE = 128
SIDE = ("own", "other")
VMEM_LIMIT = 24 * 1024 * 1024
SMALL_LIMIT = 4 * 1024 * 1024
SMEM = pl.BlockSpec(memory_space=pltpu.SMEM)
VMEM = pl.BlockSpec(memory_space=pltpu.VMEM)
ANY = pl.BlockSpec(memory_space=pl.ANY)


def pack_kernel(rows, pair_count, pair_tiles, vir, out_tiles, amp, ints, amp_out, int_out, meta):
    row_now, slab_now = lax.axis_index("row"), lax.axis_index("slab")
    amp_id = vir[lax.axis_index("col")]
    int_id = vir[row_now * lax.axis_size("slab") + slab_now]
    mt, nt, k_tiles = pair_tiles.shape[1], out_tiles.shape[0], vir.shape[0]
    count = jnp.int32(0)
    for tile in range(mt):
        meta[k_tiles + tile] = pair_tiles[0, tile]
        match = pair_tiles[0, tile] == amp_id

        @pl.when(match)
        def _():
            start = pl.multiple_of(count * TILE, TILE)
            amp_out[pl.ds(start, TILE), :] = amp[0, tile * TILE : (tile + 1) * TILE, :]

        count = count + match.astype(jnp.int32)
    count = jnp.int32(0)
    for tile in range(nt):
        meta[k_tiles + mt + tile] = out_tiles[tile]
        match = out_tiles[tile] == int_id

        @pl.when(match)
        def _():
            start = pl.multiple_of(count * TILE, TILE)
            int_out[:, pl.ds(start, TILE)] = ints[:, tile * TILE : (tile + 1) * TILE]

        count = count + match.astype(jnp.int32)
    for k in range(k_tiles):
        meta[k] = vir[k]
    meta[k_tiles + mt + nt] = pair_count[slab_now] - row_now * rows


def pack(amplitudes, integrals, pair_count, pair_sym, vir_sym, out_sym):
    rows, width = amplitudes.shape[1:]
    depth, cols = integrals.shape
    meta = pair_sym.shape[1] + vir_sym.shape[0] + out_sym.shape[0] + 1
    return pl.pallas_call(
        functools.partial(pack_kernel, rows),
        out_shape=(
            jax.ShapeDtypeStruct((rows // 2, width), jnp.bfloat16),
            jax.ShapeDtypeStruct((depth, cols // 2), jnp.bfloat16),
            jax.ShapeDtypeStruct((meta,), jnp.int32),
        ),
        in_specs=[SMEM] * 4 + [VMEM] * 2,
        out_specs=(VMEM, VMEM, SMEM),
        name="pack",
    )(pair_count, pair_sym, vir_sym, out_sym, amplitudes, integrals)


def join(arrays, passed=(), needed=(), name="join"):
    height, width = arrays[0].shape
    n, p = len(arrays), len(passed)

    def kernel(*refs):
        out = refs[n + p + len(needed)]
        for index in range(n):
            out[index * height : (index + 1) * height, :] = refs[index][...]

    return pl.pallas_call(
        kernel,
        out_shape=[jax.ShapeDtypeStruct((n * height, width), arrays[0].dtype)]
        + [jax.ShapeDtypeStruct(a.shape, a.dtype) for a in passed],
        in_specs=[VMEM] * n + [ANY] * (p + len(needed)),
        out_specs=[VMEM] + [ANY] * p,
        input_output_aliases={n + index: 1 + index for index in range(p)},
        compiler_params=pltpu.CompilerParams(vmem_limit_bytes=SMALL_LIMIT),
        name=name,
    )(*arrays, *passed, *needed)


def tile_of(step, other):
    n_row, n_slab = lax.axis_size("row"), lax.axis_size("slab")
    slab_now = lax.axis_index("slab")
    row = lax.rem(lax.axis_index("row") + step + n_row, n_row)
    return row, row * n_slab + (slab_now if other == 0 else 1 - slab_now)


def gather_tiles(pairs, meta, amps, blocks, amp_buf, int_buf, height):
    n_y = lax.axis_size("col") // 4
    core_now, hi_now, y_now = (
        lax.axis_index("col") % 2,
        lax.axis_index("col") // (2 * n_y),
        lax.axis_index("col") // 2 % n_y,
    )
    rows_ks = [tile_of(*pair) for pair in pairs]
    ids = [meta[k] for _, k in rows_ks]
    ones = sum(ids[1:], ids[0])
    zeros = len(pairs) - ones
    zero_chunks = (zeros + 1) // 2
    chunks = zero_chunks + (ones + 1) // 2

    @pl.when(zeros % 2 == 1)
    def _():
        amp_buf[zeros] = jnp.zeros(amp_buf.shape[1:], amp_buf.dtype)
        int_buf[zeros] = jnp.zeros(int_buf.shape[1:], int_buf.dtype)

    @pl.when(ones % 2 == 1)
    def _():
        last = 2 * zero_chunks + ones
        amp_buf[last] = jnp.zeros(amp_buf.shape[1:], amp_buf.dtype)
        int_buf[last] = jnp.zeros(int_buf.shape[1:], int_buf.dtype)

    nzero, none = jnp.int32(0), jnp.int32(0)
    for index, (row, k) in enumerate(rows_ks):
        spot = jnp.where(ids[index] == 1, 2 * zero_chunks + none, nzero)
        none = none + ids[index]
        nzero = nzero + 1 - ids[index]
        int_buf[spot] = blocks[index][...]
        hi = jnp.where(row // n_y == hi_now, 0, 1)
        y = lax.rem(row % n_y - y_now + n_y, n_y)
        start = pl.multiple_of((y * 2 + hi) * height, height)
        own = k % 2 == core_now

        @pl.when(own)
        def _():
            amp_buf[spot] = amps[0][pl.ds(start, height), :]

        @pl.when(jnp.logical_not(own))
        def _():
            amp_buf[spot] = amps[1][pl.ds(start, height), :]

    return zero_chunks, chunks


def chunk_product(amp_buf, int_buf, chunk):
    left = jnp.concatenate([amp_buf[2 * chunk], amp_buf[2 * chunk + 1]], axis=1)
    right = jnp.concatenate([int_buf[2 * chunk], int_buf[2 * chunk + 1]], axis=0)
    return jnp.dot(left, right, preferred_element_type=jnp.float32)


def early_kernel(pairs, n_pass, *refs):
    n = len(pairs)
    meta, amps, blocks, acc = refs[0], refs[1:3], refs[3 : 3 + n], refs[3 + n + n_pass]
    amp_buf, int_buf = refs[-2:]
    zero_chunks, chunks = gather_tiles(pairs, meta, amps, blocks, amp_buf, int_buf, amp_buf.shape[1])
    acc[...] = jnp.zeros(acc.shape, acc.dtype)

    @pl.loop(0, chunks)
    def _(chunk):
        acc[jnp.where(chunk < zero_chunks, 0, 1)] += chunk_product(amp_buf, int_buf, chunk)


def buffers(n, rows, cols):
    return [pltpu.VMEM((n + 2, rows // 2, TILE), jnp.bfloat16), pltpu.VMEM((n + 2, TILE, cols // 2), jnp.bfloat16)]


def early(rows, cols, pairs, meta, amps, blocks, passed=()):
    n, p = len(pairs), len(passed)
    return pl.pallas_call(
        functools.partial(early_kernel, pairs, p),
        out_shape=[jax.ShapeDtypeStruct((2, rows // 2, cols // 2), jnp.float32)]
        + [jax.ShapeDtypeStruct(a.shape, a.dtype) for a in passed],
        in_specs=[SMEM] + [VMEM] * (2 + n) + [ANY] * p,
        out_specs=[VMEM] + [ANY] * p,
        scratch_shapes=buffers(n, rows, cols),
        input_output_aliases={3 + n + index: 1 + index for index in range(p)},
        compiler_params=pltpu.CompilerParams(vmem_limit_bytes=VMEM_LIMIT),
        name="early_product",
    )(meta, *amps, *blocks, *passed)


def late_kernel(pairs, sizes, *refs):
    n = len(pairs)
    k_tiles, mt, nt = sizes
    meta, amps, acc_in, blocks, out = refs[0], refs[1:3], refs[3], refs[4 : 4 + n], refs[4 + n]
    amp_buf, int_buf, acc, out_buf, row_at, col_at, out_sem = refs[5 + n :]
    zero_chunks, chunks = gather_tiles(pairs, meta, amps, blocks, amp_buf, int_buf, amp_buf.shape[1])

    out_buf[...] = jnp.zeros(out_buf.shape, out_buf.dtype)
    for place, count, base in ((row_at, mt, k_tiles), (col_at, nt, k_tiles + mt)):
        nzero, none = jnp.int32(0), jnp.int32(0)
        for tile in range(count):
            is_one = meta[base + tile]
            place[jnp.where(is_one == 1, count // 2 + none, nzero)] = tile
            none = none + is_one
            nzero = nzero + 1 - is_one

    live = meta[k_tiles + mt + nt]
    for group in range(2):
        acc[...] = acc_in[group]
        first = 0 if group == 0 else zero_chunks
        last = zero_chunks if group == 0 else chunks

        @pl.loop(first, last)
        def _(chunk):
            acc[...] += chunk_product(amp_buf, int_buf, chunk)

        for r in range(mt // 2):
            tile = row_at[group * (mt // 2) + r]
            row_start = pl.multiple_of(tile * TILE, TILE)
            keep = row_start + lax.broadcasted_iota(jnp.int32, (TILE, TILE), 0) < live
            for c in range(nt // 2):
                col_start = pl.multiple_of(col_at[group * (nt // 2) + c] * TILE, TILE)
                value = acc[r * TILE : (r + 1) * TILE, c * TILE : (c + 1) * TILE]
                out_buf[pl.ds(row_start, TILE), pl.ds(col_start, TILE)] = jnp.where(keep, value, 0.0).astype(jnp.bfloat16)
            pltpu.make_async_copy(
                out_buf.at[pl.ds(row_start, TILE)],
                out.at[0, pl.ds(row_start, TILE)],
                out_sem.at[group * (mt // 2) + r],
            ).start()
    for index in range(mt):
        row_start = pl.multiple_of(row_at[index] * TILE, TILE)
        pltpu.make_async_copy(
            out_buf.at[pl.ds(row_start, TILE)], out.at[0, pl.ds(row_start, TILE)], out_sem.at[index]
        ).wait()


def late(rows, cols, k_tiles, pairs, meta, amps, acc, blocks):
    n = len(pairs)
    mt, nt = rows // TILE, cols // TILE
    return pl.pallas_call(
        functools.partial(late_kernel, pairs, (k_tiles, mt, nt)),
        out_shape=jax.ShapeDtypeStruct((1, rows, cols), jnp.bfloat16),
        in_specs=[SMEM] + [VMEM] * (3 + n),
        out_specs=ANY,
        scratch_shapes=buffers(n, rows, cols)
        + [
            pltpu.VMEM((rows // 2, cols // 2), jnp.float32),
            pltpu.VMEM((rows, cols), jnp.bfloat16),
            pltpu.SMEM((mt,), jnp.int32),
            pltpu.SMEM((nt,), jnp.int32),
            pltpu.SemaphoreType.DMA((mt,)),
        ],
        compiler_params=pltpu.CompilerParams(vmem_limit_bytes=VMEM_LIMIT),
        name="late_product",
    )(meta, *amps, acc, *blocks)


def body(amplitudes, integrals, pair_count, pair_sym, vir_sym, out_sym):
    rows, cols = amplitudes.shape[1], integrals.shape[1]
    n_row, n_col = lax.axis_size("row"), lax.axis_size("col")
    k_tiles = vir_sym.shape[0]
    n_y = n_col // 4
    amp, block, meta = pack(amplitudes, integrals, pair_count, pair_sym, vir_sym, out_sym)

    def send(a, axis, hops, name):
        with jax.named_scope(name):
            return lax.ppermute(a, axis, hops)

    def across(a):
        return send(a, "col", [(c, (c + n_col // 2) % n_col) for c in range(n_col)], "across_x")

    def swap(a):
        return send(a, "col", [(c, c ^ 1) for c in range(n_col)], "swap_cores")

    def from_y(a, d):
        hops = [((h * n_y + (y + d) % n_y) * 2 + core, (h * n_y + y) * 2 + core) for h in range(2) for y in range(n_y) for core in range(2)]
        return send(a, "col", hops, f"from_y_{d}")

    def up(a, name):
        return send(a, "row", [(i, (i + 1) % n_row) for i in range(n_row)], "up_" + name)

    def down(a, name):
        return send(a, "row", [(i, (i - 1) % n_row) for i in range(n_row)], "down_" + name)

    blocks = {(0, 0): block}
    blocks[(-1, 0)] = up(block, "own_1")
    blocks[(1, 0)] = down(block, "own_1")
    other = send(block, "slab", [(0, 1), (1, 0)], "swap_slabs")
    amp_two, blocks[(0, 1)] = join([amp, across(amp)], [other], [blocks[(-1, 0)], blocks[(1, 0)]], name="join_two")
    for step in range(1, n_row // 2 + 1):
        for slab in range(2):
            if (step < n_row // 2 or slab == 0) and (-step, slab) not in blocks:
                blocks[(-step, slab)] = up(blocks[(1 - step, slab)], f"{SIDE[slab]}_{step}")
            if (step < n_row // 2 or slab == 1) and (step, slab) not in blocks:
                blocks[(step, slab)] = down(blocks[(step - 1, slab)], f"{SIDE[slab]}_{step}")

    needed = [blocks[p] for p in ((-3, 0), (2, 0), (-2, 1), (2, 1))]
    own = join([amp_two] + [from_y(amp_two, d) for d in range(1, n_y)], needed=needed, name="join_y")[0]
    amps = [own, swap(own)]
    last = [p for p in blocks if abs(p[0]) == n_row // 2 or (abs(p[0]) == n_row // 2 - 1 and p[1] == 1)]
    first = [p for p in blocks if p not in last]
    (acc,) = early(rows, cols, first, meta, amps, [blocks[p] for p in first])
    return late(rows, cols, k_tiles, last, meta, amps, acc, [blocks[p] for p in last])


def solution(mesh):
    in_specs = (
        P("slab", "row", "col"),
        P(("row", "slab"), "col"),
        P(),
        P("slab", "row"),
        P(),
        P("col"),
    )
    out_specs = P("slab", "row", "col")
    return jax.shard_map(body, mesh=mesh, in_specs=in_specs, out_specs=out_specs, check_vma=False)
```

```python
import functools

import jax
import jax.numpy as jnp
from jax import lax
from jax.experimental import pallas as pl
from jax.experimental.pallas import tpu as pltpu
from jax.sharding import PartitionSpec as P

TILE = 128
SIDES = ("own", "other")
VMEM_LIMIT = 24 * 1024 * 1024
SMALL_LIMIT = 4 * 1024 * 1024
SMEM = pl.BlockSpec(memory_space=pltpu.SMEM)
VMEM = pl.BlockSpec(memory_space=pltpu.VMEM)
ANY = pl.BlockSpec(memory_space=pl.ANY)


def pack_kernel(rows, pair_count, pair_tiles, vir, out_tiles, amp, ints, amp_out, int_out, meta):
    row_now, slab_now = lax.axis_index("row"), lax.axis_index("slab")
    amp_id = vir[lax.axis_index("col")]
    int_id = vir[row_now * lax.axis_size("slab") + slab_now]
    mt, nt, k_tiles = pair_tiles.shape[1], out_tiles.shape[0], vir.shape[0]
    count = jnp.int32(0)
    for tile in range(mt):
        meta[k_tiles + tile] = pair_tiles[0, tile]
        match = pair_tiles[0, tile] == amp_id

        @pl.when(match)
        def _():
            start = pl.multiple_of(count * TILE, TILE)
            amp_out[pl.ds(start, TILE), :] = amp[0, tile * TILE : (tile + 1) * TILE, :]

        count = count + match.astype(jnp.int32)
    count = jnp.int32(0)
    for tile in range(nt):
        meta[k_tiles + mt + tile] = out_tiles[tile]
        match = out_tiles[tile] == int_id

        @pl.when(match)
        def _():
            start = pl.multiple_of(count * TILE, TILE)
            int_out[:, pl.ds(start, TILE)] = ints[:, tile * TILE : (tile + 1) * TILE]

        count = count + match.astype(jnp.int32)
    for k in range(k_tiles):
        meta[k] = vir[k]
    meta[k_tiles + mt + nt] = pair_count[slab_now] - row_now * rows


def pack(amplitudes, integrals, pair_count, pair_sym, vir_sym, out_sym):
    rows, width = amplitudes.shape[1:]
    depth, cols = integrals.shape
    meta = pair_sym.shape[1] + vir_sym.shape[0] + out_sym.shape[0] + 1
    return pl.pallas_call(
        functools.partial(pack_kernel, rows),
        out_shape=(
            jax.ShapeDtypeStruct((rows // 2, width), jnp.bfloat16),
            jax.ShapeDtypeStruct((depth, cols // 2), jnp.bfloat16),
            jax.ShapeDtypeStruct((meta,), jnp.int32),
        ),
        in_specs=[SMEM] * 4 + [VMEM] * 2,
        out_specs=(VMEM, VMEM, SMEM),
        name="pack",
    )(pair_count, pair_sym, vir_sym, out_sym, amplitudes, integrals)


def join(parts, needed=(), name="join"):
    parts = [part if isinstance(part, tuple) else (part, 0, part.shape[0]) for part in parts]
    n = len(parts)
    height, width = sum(part[2] for part in parts), parts[0][0].shape[1]

    def kernel(*refs):
        out = refs[n + len(needed)]
        at = 0
        for ref, (_, start, size) in zip(refs, parts):
            out[at : at + size, :] = ref[start : start + size, :]
            at += size

    return pl.pallas_call(
        kernel,
        out_shape=jax.ShapeDtypeStruct((height, width), parts[0][0].dtype),
        in_specs=[VMEM] * n + [ANY] * len(needed),
        out_specs=VMEM,
        compiler_params=pltpu.CompilerParams(vmem_limit_bytes=SMALL_LIMIT),
        name=name,
    )(*[part[0] for part in parts], *needed)


def tile_of(step, other):
    n_row, n_slab = lax.axis_size("row"), lax.axis_size("slab")
    slab_now = lax.axis_index("slab")
    row = lax.rem(lax.axis_index("row") + step + n_row, n_row)
    return row, row * n_slab + (slab_now if other == 0 else 1 - slab_now)


def gather_tiles(pairs, meta, blocks, order, int_buf, none_tile):
    ks = [tile_of(*pair)[1] for group in pairs for pair in group]
    ids = [meta[k] for k in ks]
    ones = sum(ids[1:], ids[0])
    zeros = len(ids) - ones
    zero_chunks = (zeros + 1) // 2
    chunks = zero_chunks + (ones + 1) // 2

    @pl.when(zeros % 2 == 1)
    def _():
        order[zeros] = none_tile
        int_buf[zeros] = jnp.zeros(int_buf.shape[1:], int_buf.dtype)

    @pl.when(ones % 2 == 1)
    def _():
        last = 2 * zero_chunks + ones
        order[last] = none_tile
        int_buf[last] = jnp.zeros(int_buf.shape[1:], int_buf.dtype)

    nzero, none = jnp.int32(0), jnp.int32(0)
    sources = [(ref, slot) for ref, group in zip(blocks, pairs) for slot in range(len(group))]
    for k, one, (ref, slot) in zip(ks, ids, sources):
        spot = jnp.where(one == 1, 2 * zero_chunks + none, nzero)
        none = none + one
        nzero = nzero + 1 - one
        order[spot] = k
        int_buf[spot] = ref[slot * TILE : (slot + 1) * TILE, :]
    return zero_chunks, chunks


def chunk_product(amp_all, int_buf, order, chunk):
    left = jnp.concatenate([amp_all[order[2 * chunk]], amp_all[order[2 * chunk + 1]]], axis=1)
    right = jnp.concatenate([int_buf[2 * chunk], int_buf[2 * chunk + 1]], axis=0)
    return jnp.dot(left, right, preferred_element_type=jnp.float32)


def early_kernel(pairs, n_amp, height, *refs):
    n = len(pairs)
    meta, amps, blocks = refs[0], refs[1 : 1 + n_amp], refs[1 + n_amp : 1 + n_amp + n]
    acc, amp_all, int_buf, order = refs[1 + n_amp + n :]
    col = lax.axis_index("col")
    n_y = amps[0].shape[0] // (2 * height)
    hi_now, y_now, core_now = col // (2 * n_y), col // 2 % n_y, col % 2
    for core in range(2):
        for y in range(n_y):
            for hi in range(2):
                k = ((hi_now if hi == 0 else 1 - hi_now) * n_y + jnp.bitwise_xor(y_now, y)) * 2 + (
                    core_now if core == 0 else 1 - core_now
                )
                at = (2 * y + hi) * height
                amp_all[k] = amps[core][at : at + height, :]
    none_tile = amp_all.shape[0] - 1
    amp_all[none_tile] = jnp.zeros(amp_all.shape[1:], amp_all.dtype)
    zero_chunks, chunks = gather_tiles(pairs, meta, blocks, order, int_buf, none_tile)
    acc[...] = jnp.zeros(acc.shape, acc.dtype)

    @pl.loop(0, chunks)
    def _(chunk):
        acc[jnp.where(chunk < zero_chunks, 0, 1)] += chunk_product(amp_all, int_buf, order, chunk)


def buffers(pairs, cols):
    n = sum(len(group) for group in pairs) + 2
    return [pltpu.VMEM((n, TILE, cols // 2), jnp.bfloat16), pltpu.SMEM((n,), jnp.int32)]


def early(rows, cols, k_tiles, pairs, meta, amps, blocks):
    n, n_amp = len(pairs), len(amps)
    return pl.pallas_call(
        functools.partial(early_kernel, pairs, n_amp, rows // 2),
        out_shape=(
            jax.ShapeDtypeStruct((2, rows // 2, cols // 2), jnp.float32),
            jax.ShapeDtypeStruct((k_tiles + 1, rows // 2, TILE), jnp.bfloat16),
        ),
        in_specs=[SMEM] + [VMEM] * (n_amp + n),
        out_specs=(VMEM, VMEM),
        scratch_shapes=buffers(pairs, cols),
        compiler_params=pltpu.CompilerParams(vmem_limit_bytes=VMEM_LIMIT),
        name="early_product",
    )(meta, *amps, *blocks)


def late_kernel(pairs, sizes, *refs):
    n = len(pairs)
    k_tiles, mt, nt = sizes
    meta, acc_in, amp_all, blocks, out = refs[0], refs[1], refs[2], refs[3 : 3 + n], refs[3 + n]
    int_buf, order, acc, out_buf, row_at, col_at, out_sem = refs[4 + n :]
    zero_chunks, chunks = gather_tiles(pairs, meta, blocks, order, int_buf, k_tiles)

    out_buf[...] = jnp.zeros(out_buf.shape, out_buf.dtype)
    for place, count, base in ((row_at, mt, k_tiles), (col_at, nt, k_tiles + mt)):
        nzero, none = jnp.int32(0), jnp.int32(0)
        for tile in range(count):
            is_one = meta[base + tile]
            place[jnp.where(is_one == 1, count // 2 + none, nzero)] = tile
            none = none + is_one
            nzero = nzero + 1 - is_one

    live = meta[k_tiles + mt + nt]
    for group in range(2):
        acc[...] = acc_in[group]
        first = 0 if group == 0 else zero_chunks
        last = zero_chunks if group == 0 else chunks

        @pl.loop(first, last)
        def _(chunk):
            acc[...] += chunk_product(amp_all, int_buf, order, chunk)

        for r in range(mt // 2):
            tile = row_at[group * (mt // 2) + r]
            row_start = pl.multiple_of(tile * TILE, TILE)
            keep = row_start + lax.broadcasted_iota(jnp.int32, (TILE, TILE), 0) < live
            for c in range(nt // 2):
                col_start = pl.multiple_of(col_at[group * (nt // 2) + c] * TILE, TILE)
                value = acc[r * TILE : (r + 1) * TILE, c * TILE : (c + 1) * TILE]
                out_buf[pl.ds(row_start, TILE), pl.ds(col_start, TILE)] = jnp.where(keep, value, 0.0).astype(jnp.bfloat16)
            pltpu.make_async_copy(
                out_buf.at[pl.ds(row_start, TILE)],
                out.at[0, pl.ds(row_start, TILE)],
                out_sem.at[group * (mt // 2) + r],
            ).start()
    for index in range(mt):
        row_start = pl.multiple_of(row_at[index] * TILE, TILE)
        pltpu.make_async_copy(
            out_buf.at[pl.ds(row_start, TILE)], out.at[0, pl.ds(row_start, TILE)], out_sem.at[index]
        ).wait()


def late(rows, cols, k_tiles, pairs, meta, acc, amp_all, blocks):
    n = len(pairs)
    mt, nt = rows // TILE, cols // TILE
    return pl.pallas_call(
        functools.partial(late_kernel, pairs, (k_tiles, mt, nt)),
        out_shape=jax.ShapeDtypeStruct((1, rows, cols), jnp.bfloat16),
        in_specs=[SMEM] + [VMEM] * (2 + n),
        out_specs=ANY,
        scratch_shapes=buffers(pairs, cols)
        + [
            pltpu.VMEM((rows // 2, cols // 2), jnp.float32),
            pltpu.VMEM((rows, cols), jnp.bfloat16),
            pltpu.SMEM((mt,), jnp.int32),
            pltpu.SMEM((nt,), jnp.int32),
            pltpu.SemaphoreType.DMA((mt,)),
        ],
        compiler_params=pltpu.CompilerParams(vmem_limit_bytes=VMEM_LIMIT),
        name="late_product",
    )(meta, acc, amp_all, *blocks)


def body(amplitudes, integrals, pair_count, pair_sym, vir_sym, out_sym):
    rows, cols = amplitudes.shape[1], integrals.shape[1]
    n_row, n_col = lax.axis_size("row"), lax.axis_size("col")
    k_tiles = vir_sym.shape[0]
    n_y = n_col // 4
    amp, block, meta = pack(amplitudes, integrals, pair_count, pair_sym, vir_sym, out_sym)

    def send(a, axis, hops, name):
        with jax.named_scope(name):
            return lax.ppermute(a, axis, hops)

    def across(a):
        return send(a, "col", [(c, (c + n_col // 2) % n_col) for c in range(n_col)], "across_x")

    def swap(a):
        return send(a, "col", [(c, c ^ 1) for c in range(n_col)], "swap_cores")

    def from_y(a, d):
        hops = [(c, c ^ (2 * d)) for c in range(n_col)]
        return send(a, "col", hops, f"from_y_{d}")

    def up(a, name):
        return send(a, "row", [(i, (i + 1) % n_row) for i in range(n_row)], "up_" + name)

    def down(a, name):
        return send(a, "row", [(i, (i - 1) % n_row) for i in range(n_row)], "down_" + name)

    def swap_slabs(a, step):
        return send(a, "slab", [(0, 1), (1, 0)], f"swap_slabs_{step}")

    half = TILE // 2
    other = swap_slabs(block, 0)
    below, above = up(block, "own_1"), down(block, "own_1")
    amp_two = join([amp, across(amp)], needed=[other], name="join_two")
    both = join([below, above], needed=[amp_two], name="join_own_1")
    both_1, others_1 = both, swap_slabs(both, 1)
    below, above = up(join([(both, 0, TILE)], name="split"), "own_2"), down(join([(both, TILE, TILE)], name="split"), "own_2")
    amps = {0: amp_two, 1: from_y(amp_two, 1), 3: from_y(amp_two, 3)}
    both_2 = join([below, above], name="join_own_2")
    others_2 = swap_slabs(both_2, 2)
    below, above = up(join([(both_2, 0, TILE)], name="split"), "own_3"), down(join([(both_2, TILE, TILE)], name="split"), "own_3")
    amps[2] = from_y(join([amp_two], needed=[amps[1], amps[3], others_1], name="hold"), 2)
    both_3 = join([below, above], needed=[amps[1], amps[3]], name="join_own_3")
    low = up(join([(both_3, 0, half)], name="split"), "own_half")
    high = down(join([(both_3, TILE + half, half)], name="split"), "own_half")
    own_4 = join([low, high], needed=[others_2], name="join_own_4")
    other_4 = swap_slabs(own_4, 4)
    other_below = up(join([(others_2, 0, TILE)], name="split"), "other_3")
    other_above = down(join([(others_2, TILE, TILE)], name="split"), "other_3")

    own = join([amps[y] for y in range(n_y)], needed=[own_4], name="join_y")
    amps = [own, swap(own)]
    first = {
        ((0, 0),): block,
        ((0, 1),): other,
        ((-1, 0), (1, 0)): both_1,
        ((-1, 1), (1, 1)): others_1,
        ((-2, 0), (2, 0)): both_2,
        ((-2, 1), (2, 1)): others_2,
        ((-3, 0), (3, 0)): both_3,
    }
    last = {((-4, 0),): own_4, ((-3, 1),): other_below, ((3, 1),): other_above, ((-4, 1),): other_4}
    acc, amp_all = early(rows, cols, k_tiles, list(first), meta, amps, list(first.values()))
    return late(rows, cols, k_tiles, list(last), meta, acc, amp_all, list(last.values()))


def solution(mesh):
    in_specs = (
        P("slab", "row", "col"),
        P(("row", "slab"), "col"),
        P(),
        P("slab", "row"),
        P(),
        P("col"),
    )
    out_specs = P("slab", "row", "col")
    return jax.shard_map(body, mesh=mesh, in_specs=in_specs, out_specs=out_specs, check_vma=False)
```

```python
import functools

import jax
import jax.numpy as jnp
from jax import lax
from jax.experimental import pallas as pl
from jax.experimental.pallas import tpu as pltpu
from jax.sharding import PartitionSpec as P

TILE = 128
SIDES = ("own", "other")
VMEM_LIMIT = 24 * 1024 * 1024
SMALL_LIMIT = 4 * 1024 * 1024
SMEM = pl.BlockSpec(memory_space=pltpu.SMEM)
VMEM = pl.BlockSpec(memory_space=pltpu.VMEM)
ANY = pl.BlockSpec(memory_space=pl.ANY)


def pack_kernel(rows, pair_count, pair_tiles, vir, out_tiles, amp, ints, amp_out, int_out, meta):
    row_now, slab_now = lax.axis_index("row"), lax.axis_index("slab")
    amp_id = vir[lax.axis_index("col")]
    int_id = vir[row_now * lax.axis_size("slab") + slab_now]
    mt, nt, k_tiles = pair_tiles.shape[1], out_tiles.shape[0], vir.shape[0]
    count = jnp.int32(0)
    for tile in range(mt):
        meta[k_tiles + tile] = pair_tiles[0, tile]
        match = pair_tiles[0, tile] == amp_id

        @pl.when(match)
        def _():
            start = pl.multiple_of(count * TILE, TILE)
            amp_out[pl.ds(start, TILE), :] = amp[0, tile * TILE : (tile + 1) * TILE, :]

        count = count + match.astype(jnp.int32)
    count = jnp.int32(0)
    for tile in range(nt):
        meta[k_tiles + mt + tile] = out_tiles[tile]
        match = out_tiles[tile] == int_id

        @pl.when(match)
        def _():
            start = pl.multiple_of(count * TILE, TILE)
            int_out[:, pl.ds(start, TILE)] = ints[:, tile * TILE : (tile + 1) * TILE]

        count = count + match.astype(jnp.int32)
    for k in range(k_tiles):
        meta[k] = vir[k]
    meta[k_tiles + mt + nt] = pair_count[slab_now] - row_now * rows


def pack(amplitudes, integrals, pair_count, pair_sym, vir_sym, out_sym):
    rows, width = amplitudes.shape[1:]
    depth, cols = integrals.shape
    meta = pair_sym.shape[1] + vir_sym.shape[0] + out_sym.shape[0] + 1
    return pl.pallas_call(
        functools.partial(pack_kernel, rows),
        out_shape=(
            jax.ShapeDtypeStruct((rows // 2, width), jnp.bfloat16),
            jax.ShapeDtypeStruct((depth, cols // 2), jnp.bfloat16),
            jax.ShapeDtypeStruct((meta,), jnp.int32),
        ),
        in_specs=[SMEM] * 4 + [VMEM] * 2,
        out_specs=(VMEM, VMEM, SMEM),
        name="pack",
    )(pair_count, pair_sym, vir_sym, out_sym, amplitudes, integrals)


def join(parts, needed=(), name="join", flops=0):
    parts = [part if isinstance(part, tuple) else (part, 0, part.shape[0]) for part in parts]
    n = len(parts)
    height, width = sum(part[2] for part in parts), parts[0][0].shape[1]

    def kernel(*refs):
        out = refs[n + len(needed)]
        at = 0
        for ref, (_, start, size) in zip(refs, parts):
            out[at : at + size, :] = ref[start : start + size, :]
            at += size

    return pl.pallas_call(
        kernel,
        out_shape=jax.ShapeDtypeStruct((height, width), parts[0][0].dtype),
        in_specs=[VMEM] * n + [ANY] * len(needed),
        out_specs=VMEM,
        compiler_params=pltpu.CompilerParams(vmem_limit_bytes=SMALL_LIMIT),
        cost_estimate=pl.CostEstimate(flops=flops, bytes_accessed=0, transcendentals=0) if flops else None,
        name=name,
    )(*[part[0] for part in parts], *needed)


def tile_of(step, other):
    n_row, n_slab = lax.axis_size("row"), lax.axis_size("slab")
    slab_now = lax.axis_index("slab")
    row = lax.rem(lax.axis_index("row") + step + n_row, n_row)
    return row, row * n_slab + (slab_now if other == 0 else 1 - slab_now)


def gather_tiles(pairs, meta, blocks, order, int_buf, none_tile):
    ks = [tile_of(*pair)[1] for group in pairs for pair in group]
    ids = [meta[k] for k in ks]
    ones = sum(ids[1:], ids[0])
    zeros = len(ids) - ones
    zero_chunks = (zeros + 1) // 2
    chunks = zero_chunks + (ones + 1) // 2

    @pl.when(zeros % 2 == 1)
    def _():
        order[zeros] = none_tile
        int_buf[zeros] = jnp.zeros(int_buf.shape[1:], int_buf.dtype)

    @pl.when(ones % 2 == 1)
    def _():
        last = 2 * zero_chunks + ones
        order[last] = none_tile
        int_buf[last] = jnp.zeros(int_buf.shape[1:], int_buf.dtype)

    nzero, none = jnp.int32(0), jnp.int32(0)
    sources = [(ref, slot) for ref, group in zip(blocks, pairs) for slot in range(len(group))]
    for k, one, (ref, slot) in zip(ks, ids, sources):
        spot = jnp.where(one == 1, 2 * zero_chunks + none, nzero)
        none = none + one
        nzero = nzero + 1 - one
        order[spot] = k
        int_buf[spot] = ref[slot * TILE : (slot + 1) * TILE, :]
    return zero_chunks, chunks


def chunk_product(amp_all, int_buf, order, chunk):
    left = jnp.concatenate([amp_all[order[2 * chunk]], amp_all[order[2 * chunk + 1]]], axis=1)
    right = jnp.concatenate([int_buf[2 * chunk], int_buf[2 * chunk + 1]], axis=0)
    return jnp.dot(left, right, preferred_element_type=jnp.float32)


def early_kernel(pairs, n_amp, height, *refs):
    n = len(pairs)
    meta, amps, blocks = refs[0], refs[1 : 1 + n_amp], refs[1 + n_amp : 1 + n_amp + n]
    acc, amp_all, int_buf, order = refs[1 + n_amp + n :]
    col = lax.axis_index("col")
    n_y = amps[0].shape[0] // (2 * height)
    hi_now, y_now, core_now = col // (2 * n_y), col // 2 % n_y, col % 2
    for core in range(2):
        for y in range(n_y):
            for hi in range(2):
                k = ((hi_now if hi == 0 else 1 - hi_now) * n_y + jnp.bitwise_xor(y_now, y)) * 2 + (
                    core_now if core == 0 else 1 - core_now
                )
                at = (2 * y + hi) * height
                amp_all[k] = amps[core][at : at + height, :]
    none_tile = amp_all.shape[0] - 1
    amp_all[none_tile] = jnp.zeros(amp_all.shape[1:], amp_all.dtype)
    zero_chunks, chunks = gather_tiles(pairs, meta, blocks, order, int_buf, none_tile)
    acc[...] = jnp.zeros(acc.shape, acc.dtype)

    @pl.loop(0, chunks)
    def _(chunk):
        acc[jnp.where(chunk < zero_chunks, 0, 1)] += chunk_product(amp_all, int_buf, order, chunk)


def buffers(pairs, cols):
    n = sum(len(group) for group in pairs) + 2
    return [pltpu.VMEM((n, TILE, cols // 2), jnp.bfloat16), pltpu.SMEM((n,), jnp.int32)]


def early(rows, cols, k_tiles, pairs, meta, amps, blocks):
    n, n_amp = len(pairs), len(amps)
    return pl.pallas_call(
        functools.partial(early_kernel, pairs, n_amp, rows // 2),
        out_shape=(
            jax.ShapeDtypeStruct((2, rows // 2, cols // 2), jnp.float32),
            jax.ShapeDtypeStruct((k_tiles + 1, rows // 2, TILE), jnp.bfloat16),
        ),
        in_specs=[SMEM] + [VMEM] * (n_amp + n),
        out_specs=(VMEM, VMEM),
        scratch_shapes=buffers(pairs, cols),
        compiler_params=pltpu.CompilerParams(vmem_limit_bytes=VMEM_LIMIT),
        name="early_product",
    )(meta, *amps, *blocks)


def late_kernel(pairs, sizes, *refs):
    n = len(pairs)
    k_tiles, mt, nt = sizes
    meta, acc_in, amp_all, blocks, out = refs[0], refs[1], refs[2], refs[3 : 3 + n], refs[3 + n]
    int_buf, order, acc, out_buf, row_at, col_at, out_sem = refs[4 + n :]
    zero_chunks, chunks = gather_tiles(pairs, meta, blocks, order, int_buf, k_tiles)

    for place, count, base in ((row_at, mt, k_tiles), (col_at, nt, k_tiles + mt)):
        nzero, none = jnp.int32(0), jnp.int32(0)
        for tile in range(count):
            is_one = meta[base + tile]
            place[jnp.where(is_one == 1, count // 2 + none, nzero)] = tile
            none = none + is_one
            nzero = nzero + 1 - is_one

    live = meta[k_tiles + mt + nt]
    for group in range(2):
        first = 0 if group == 0 else zero_chunks
        last = zero_chunks if group == 0 else chunks

        @pl.when(first == last)
        def _():
            acc[...] = acc_in[group]

        @pl.when(first < last)
        def _():
            acc[...] = acc_in[group] + chunk_product(amp_all, int_buf, order, first)

        @pl.loop(first + 1, last)
        def _(chunk):
            acc[...] += chunk_product(amp_all, int_buf, order, chunk)

        for r in range(mt // 2):
            tile = row_at[group * (mt // 2) + r]
            row_start = pl.multiple_of(tile * TILE, TILE)
            keep = row_start + lax.broadcasted_iota(jnp.int32, (TILE, TILE), 0) < live
            for c in range(nt // 2):
                col_start = pl.multiple_of(col_at[group * (nt // 2) + c] * TILE, TILE)
                value = acc[r * TILE : (r + 1) * TILE, c * TILE : (c + 1) * TILE]
                out_buf[pl.ds(row_start, TILE), pl.ds(col_start, TILE)] = jnp.where(keep, value, 0.0).astype(jnp.bfloat16)
                empty = pl.multiple_of(col_at[(1 - group) * (nt // 2) + c] * TILE, TILE)
                out_buf[pl.ds(row_start, TILE), pl.ds(empty, TILE)] = jnp.zeros((TILE, TILE), jnp.bfloat16)
            pltpu.make_async_copy(
                out_buf.at[pl.ds(row_start, TILE)],
                out.at[0, pl.ds(row_start, TILE)],
                out_sem.at[group * (mt // 2) + r],
            ).start()
    for index in range(mt):
        row_start = pl.multiple_of(row_at[index] * TILE, TILE)
        pltpu.make_async_copy(
            out_buf.at[pl.ds(row_start, TILE)], out.at[0, pl.ds(row_start, TILE)], out_sem.at[index]
        ).wait()


def late(rows, cols, k_tiles, pairs, meta, acc, amp_all, blocks):
    n = len(pairs)
    mt, nt = rows // TILE, cols // TILE
    return pl.pallas_call(
        functools.partial(late_kernel, pairs, (k_tiles, mt, nt)),
        out_shape=jax.ShapeDtypeStruct((1, rows, cols), jnp.bfloat16),
        in_specs=[SMEM] + [VMEM] * (2 + n),
        out_specs=ANY,
        scratch_shapes=buffers(pairs, cols)
        + [
            pltpu.VMEM((rows // 2, cols // 2), jnp.float32),
            pltpu.VMEM((rows, cols), jnp.bfloat16),
            pltpu.SMEM((mt,), jnp.int32),
            pltpu.SMEM((nt,), jnp.int32),
            pltpu.SemaphoreType.DMA((mt,)),
        ],
        compiler_params=pltpu.CompilerParams(vmem_limit_bytes=VMEM_LIMIT),
        name="late_product",
    )(meta, acc, amp_all, *blocks)


def body(amplitudes, integrals, pair_count, pair_sym, vir_sym, out_sym):
    rows, cols = amplitudes.shape[1], integrals.shape[1]
    n_row, n_col = lax.axis_size("row"), lax.axis_size("col")
    k_tiles = vir_sym.shape[0]
    n_y = n_col // 4
    amp, block, meta = pack(amplitudes, integrals, pair_count, pair_sym, vir_sym, out_sym)

    def send(a, axis, hops, name):
        with jax.named_scope(name):
            return lax.ppermute(a, axis, hops)

    def across(a):
        return send(a, "col", [(c, (c + n_col // 2) % n_col) for c in range(n_col)], "across_x")

    def swap(a):
        return send(a, "col", [(c, c ^ 1) for c in range(n_col)], "swap_cores")

    def from_y(a, d):
        hops = [(c, c ^ (2 * d)) for c in range(n_col)]
        return send(a, "col", hops, f"from_y_{d}")

    def up(a, name):
        return send(a, "row", [(i, (i + 1) % n_row) for i in range(n_row)], "up_" + name)

    def down(a, name):
        return send(a, "row", [(i, (i - 1) % n_row) for i in range(n_row)], "down_" + name)

    def swap_slabs(a, step):
        return send(a, "slab", [(0, 1), (1, 0)], f"swap_slabs_{step}")

    half = TILE // 2
    other = swap_slabs(block, 0)
    below, above = up(block, "own_1"), down(block, "own_1")
    amp_two = join([join([amp], name="hold"), across(amp)], needed=[other], name="join_two", flops=3000000000)
    both = join([below, above], needed=[amp_two], name="join_own_1", flops=0)
    both_1, others_1 = both, swap_slabs(both, 1)
    below, above = up(join([(both, 0, TILE)], name="split"), "own_2"), down(join([(both, TILE, TILE)], name="split"), "own_2")
    amps = {0: amp_two, 1: from_y(amp_two, 1), 3: from_y(amp_two, 3)}
    both_2 = join([below, above], name="join_own_2", flops=5000000000)
    others_2 = swap_slabs(both_2, 2)
    below, above = up(join([(both_2, 0, TILE)], name="split"), "own_3"), down(join([(both_2, TILE, TILE)], name="split"), "own_3")
    amps[2] = from_y(join([amp_two], needed=[amps[1], amps[3]], name="hold"), 2)
    both_3 = join([below, above], needed=[others_1], name="join_own_3", flops=5000000000)
    low = up(join([(both_3, 0, half)], name="split"), "own_half")
    high = down(join([(both_3, TILE + half, half)], name="split"), "own_half")
    own_4 = join([low, high], needed=[others_2], name="join_own_4")
    other_4 = swap_slabs(own_4, 4)
    other_below = up(join([(others_2, 0, TILE)], name="split"), "other_3")
    other_above = down(join([(others_2, TILE, TILE)], name="split"), "other_3")

    own = join([amps[y] for y in range(n_y)], needed=[own_4], name="join_y")
    amps = [own, swap(own)]
    first = {
        ((0, 0),): block,
        ((0, 1),): other,
        ((-1, 0), (1, 0)): both_1,
        ((-1, 1), (1, 1)): others_1,
        ((-2, 0), (2, 0)): both_2,
        ((-2, 1), (2, 1)): others_2,
        ((-3, 0), (3, 0)): both_3,
    }
    last = {((-4, 0),): own_4, ((-3, 1),): other_below, ((3, 1),): other_above, ((-4, 1),): other_4}
    acc, amp_all = early(rows, cols, k_tiles, list(first), meta, amps, list(first.values()))
    return late(rows, cols, k_tiles, list(last), meta, acc, amp_all, list(last.values()))


def solution(mesh):
    in_specs = (
        P("slab", "row", "col"),
        P(("row", "slab"), "col"),
        P(),
        P("slab", "row"),
        P(),
        P("col"),
    )
    out_specs = P("slab", "row", "col")
    return jax.shard_map(body, mesh=mesh, in_specs=in_specs, out_specs=out_specs, check_vma=False)
```

```python
import functools

import jax
import jax.numpy as jnp
from jax import lax
from jax.experimental import pallas as pl
from jax.experimental.pallas import tpu as pltpu
from jax.sharding import PartitionSpec as P

TILE = 128
SIDES = ("own", "other")
VMEM_LIMIT = 24 * 1024 * 1024
SMALL_LIMIT = 4 * 1024 * 1024
SMEM = pl.BlockSpec(memory_space=pltpu.SMEM)
VMEM = pl.BlockSpec(memory_space=pltpu.VMEM)
ANY = pl.BlockSpec(memory_space=pl.ANY)


def pack_kernel(rows, pair_count, pair_tiles, vir, out_tiles, amp, ints, amp_out, int_out, meta):
    row_now, slab_now = lax.axis_index("row"), lax.axis_index("slab")
    amp_id = vir[lax.axis_index("col")]
    int_id = vir[row_now * lax.axis_size("slab") + slab_now]
    mt, nt, k_tiles = pair_tiles.shape[1], out_tiles.shape[0], vir.shape[0]
    count = jnp.int32(0)
    for tile in range(mt):
        meta[k_tiles + tile] = pair_tiles[0, tile]
        match = pair_tiles[0, tile] == amp_id

        @pl.when(match)
        def _():
            start = pl.multiple_of(count * TILE, TILE)
            amp_out[pl.ds(start, TILE), :] = amp[0, tile * TILE : (tile + 1) * TILE, :]

        count = count + match.astype(jnp.int32)
    count = jnp.int32(0)
    for tile in range(nt):
        meta[k_tiles + mt + tile] = out_tiles[tile]
        match = out_tiles[tile] == int_id

        @pl.when(match)
        def _():
            start = pl.multiple_of(count * TILE, TILE)
            int_out[:, pl.ds(start, TILE)] = ints[:, tile * TILE : (tile + 1) * TILE]

        count = count + match.astype(jnp.int32)
    for k in range(k_tiles):
        meta[k] = vir[k]
    meta[k_tiles + mt + nt] = pair_count[slab_now] - row_now * rows


def pack(amplitudes, integrals, pair_count, pair_sym, vir_sym, out_sym):
    rows, width = amplitudes.shape[1:]
    depth, cols = integrals.shape
    meta = pair_sym.shape[1] + vir_sym.shape[0] + out_sym.shape[0] + 1
    return pl.pallas_call(
        functools.partial(pack_kernel, rows),
        out_shape=(
            jax.ShapeDtypeStruct((rows // 2, width), jnp.bfloat16),
            jax.ShapeDtypeStruct((depth, cols // 2), jnp.bfloat16),
            jax.ShapeDtypeStruct((meta,), jnp.int32),
        ),
        in_specs=[SMEM] * 4 + [VMEM] * 2,
        out_specs=(VMEM, VMEM, SMEM),
        name="pack",
    )(pair_count, pair_sym, vir_sym, out_sym, amplitudes, integrals)


def join(parts, needed=(), name="join", flops=0):
    parts = [part if isinstance(part, tuple) else (part, 0, part.shape[0]) for part in parts]
    n = len(parts)
    height, width = sum(part[2] for part in parts), parts[0][0].shape[1]

    def kernel(*refs):
        out = refs[n + len(needed)]
        at = 0
        for ref, (_, start, size) in zip(refs, parts):
            out[at : at + size, :] = ref[start : start + size, :]
            at += size

    return pl.pallas_call(
        kernel,
        out_shape=jax.ShapeDtypeStruct((height, width), parts[0][0].dtype),
        in_specs=[VMEM] * n + [ANY] * len(needed),
        out_specs=VMEM,
        compiler_params=pltpu.CompilerParams(vmem_limit_bytes=SMALL_LIMIT),
        cost_estimate=pl.CostEstimate(flops=flops, bytes_accessed=0, transcendentals=0) if flops else None,
        name=name,
    )(*[part[0] for part in parts], *needed)


def tile_of(step, other):
    n_row, n_slab = lax.axis_size("row"), lax.axis_size("slab")
    slab_now = lax.axis_index("slab")
    row = lax.rem(lax.axis_index("row") + step + n_row, n_row)
    return row, row * n_slab + (slab_now if other == 0 else 1 - slab_now)


def gather_tiles(pairs, meta, blocks, order, int_buf, none_tile):
    ks = [tile_of(*pair)[1] for group in pairs for pair in group]
    ids = [meta[k] for k in ks]
    ones = sum(ids[1:], ids[0])
    zeros = len(ids) - ones
    zero_chunks = (zeros + 1) // 2
    chunks = zero_chunks + (ones + 1) // 2

    @pl.when(zeros % 2 == 1)
    def _():
        order[zeros] = none_tile
        int_buf[zeros] = jnp.zeros(int_buf.shape[1:], int_buf.dtype)

    @pl.when(ones % 2 == 1)
    def _():
        last = 2 * zero_chunks + ones
        order[last] = none_tile
        int_buf[last] = jnp.zeros(int_buf.shape[1:], int_buf.dtype)

    nzero, none = jnp.int32(0), jnp.int32(0)
    sources = [(ref, slot) for ref, group in zip(blocks, pairs) for slot in range(len(group))]
    for k, one, (ref, slot) in zip(ks, ids, sources):
        spot = jnp.where(one == 1, 2 * zero_chunks + none, nzero)
        none = none + one
        nzero = nzero + 1 - one
        order[spot] = k
        int_buf[spot] = ref[slot * TILE : (slot + 1) * TILE, :]
    return zero_chunks, chunks


def chunk_product(amp_all, int_buf, order, chunk):
    left = jnp.concatenate([amp_all[order[2 * chunk]], amp_all[order[2 * chunk + 1]]], axis=1)
    right = jnp.concatenate([int_buf[2 * chunk], int_buf[2 * chunk + 1]], axis=0)
    return jnp.dot(left, right, preferred_element_type=jnp.float32)


def early_kernel(pairs, n_amp, height, *refs):
    n = len(pairs)
    meta, amps, blocks = refs[0], refs[1 : 1 + n_amp], refs[1 + n_amp : 1 + n_amp + n]
    acc, amp_all, int_buf, order = refs[1 + n_amp + n :]
    col = lax.axis_index("col")
    n_y = n_amp // 2
    hi_now, y_now, core_now = col // (2 * n_y), col // 2 % n_y, col % 2
    for core in range(2):
        for y in range(n_y):
            for hi in range(2):
                k = ((hi_now if hi == 0 else 1 - hi_now) * n_y + jnp.bitwise_xor(y_now, y)) * 2 + (
                    core_now if core == 0 else 1 - core_now
                )
                amp_all[k] = amps[core * n_y + y][hi * height : (hi + 1) * height, :]
    none_tile = amp_all.shape[0] - 1
    amp_all[none_tile] = jnp.zeros(amp_all.shape[1:], amp_all.dtype)
    zero_chunks, chunks = gather_tiles(pairs, meta, blocks, order, int_buf, none_tile)
    acc[...] = jnp.zeros(acc.shape, acc.dtype)

    @pl.loop(0, chunks)
    def _(chunk):
        acc[jnp.where(chunk < zero_chunks, 0, 1)] += chunk_product(amp_all, int_buf, order, chunk)


def buffers(pairs, cols):
    n = sum(len(group) for group in pairs) + 2
    return [pltpu.VMEM((n, TILE, cols // 2), jnp.bfloat16), pltpu.SMEM((n,), jnp.int32)]


def early(rows, cols, k_tiles, pairs, meta, amps, blocks):
    n, n_amp = len(pairs), len(amps)
    return pl.pallas_call(
        functools.partial(early_kernel, pairs, n_amp, rows // 2),
        out_shape=(
            jax.ShapeDtypeStruct((2, rows // 2, cols // 2), jnp.float32),
            jax.ShapeDtypeStruct((k_tiles + 1, rows // 2, TILE), jnp.bfloat16),
        ),
        in_specs=[SMEM] + [VMEM] * (n_amp + n),
        out_specs=(VMEM, VMEM),
        scratch_shapes=buffers(pairs, cols),
        compiler_params=pltpu.CompilerParams(vmem_limit_bytes=VMEM_LIMIT),
        name="early_product",
    )(meta, *amps, *blocks)


def late_kernel(pairs, sizes, *refs):
    n = len(pairs)
    k_tiles, mt, nt = sizes
    meta, acc_in, amp_all, blocks, out = refs[0], refs[1], refs[2], refs[3 : 3 + n], refs[3 + n]
    int_buf, order, acc, out_buf, row_at, col_at, out_sem = refs[4 + n :]
    zero_chunks, chunks = gather_tiles(pairs, meta, blocks, order, int_buf, k_tiles)

    for place, count, base in ((row_at, mt, k_tiles), (col_at, nt, k_tiles + mt)):
        nzero, none = jnp.int32(0), jnp.int32(0)
        for tile in range(count):
            is_one = meta[base + tile]
            place[jnp.where(is_one == 1, count // 2 + none, nzero)] = tile
            none = none + is_one
            nzero = nzero + 1 - is_one

    live = meta[k_tiles + mt + nt]
    for group in range(2):
        first = 0 if group == 0 else zero_chunks
        last = zero_chunks if group == 0 else chunks

        @pl.when(first == last)
        def _():
            acc[...] = acc_in[group]

        @pl.when(first < last)
        def _():
            acc[...] = acc_in[group] + chunk_product(amp_all, int_buf, order, first)

        @pl.loop(first + 1, last)
        def _(chunk):
            acc[...] += chunk_product(amp_all, int_buf, order, chunk)

        for r in range(mt // 2):
            tile = row_at[group * (mt // 2) + r]
            row_start = pl.multiple_of(tile * TILE, TILE)
            keep = row_start + lax.broadcasted_iota(jnp.int32, (TILE, TILE), 0) < live
            for c in range(nt // 2):
                col_start = pl.multiple_of(col_at[group * (nt // 2) + c] * TILE, TILE)
                value = acc[r * TILE : (r + 1) * TILE, c * TILE : (c + 1) * TILE]
                out_buf[pl.ds(row_start, TILE), pl.ds(col_start, TILE)] = jnp.where(keep, value, 0.0).astype(jnp.bfloat16)
                empty = pl.multiple_of(col_at[(1 - group) * (nt // 2) + c] * TILE, TILE)
                out_buf[pl.ds(row_start, TILE), pl.ds(empty, TILE)] = jnp.zeros((TILE, TILE), jnp.bfloat16)
            pltpu.make_async_copy(
                out_buf.at[pl.ds(row_start, TILE)],
                out.at[0, pl.ds(row_start, TILE)],
                out_sem.at[group * (mt // 2) + r],
            ).start()
    for index in range(mt):
        row_start = pl.multiple_of(row_at[index] * TILE, TILE)
        pltpu.make_async_copy(
            out_buf.at[pl.ds(row_start, TILE)], out.at[0, pl.ds(row_start, TILE)], out_sem.at[index]
        ).wait()


def late(rows, cols, k_tiles, pairs, meta, acc, amp_all, blocks):
    n = len(pairs)
    mt, nt = rows // TILE, cols // TILE
    return pl.pallas_call(
        functools.partial(late_kernel, pairs, (k_tiles, mt, nt)),
        out_shape=jax.ShapeDtypeStruct((1, rows, cols), jnp.bfloat16),
        in_specs=[SMEM] + [VMEM] * (2 + n),
        out_specs=ANY,
        scratch_shapes=buffers(pairs, cols)
        + [
            pltpu.VMEM((rows // 2, cols // 2), jnp.float32),
            pltpu.VMEM((rows, cols), jnp.bfloat16),
            pltpu.SMEM((mt,), jnp.int32),
            pltpu.SMEM((nt,), jnp.int32),
            pltpu.SemaphoreType.DMA((mt,)),
        ],
        compiler_params=pltpu.CompilerParams(vmem_limit_bytes=VMEM_LIMIT),
        name="late_product",
    )(meta, acc, amp_all, *blocks)


def body(amplitudes, integrals, pair_count, pair_sym, vir_sym, out_sym):
    rows, cols = amplitudes.shape[1], integrals.shape[1]
    n_row, n_col = lax.axis_size("row"), lax.axis_size("col")
    k_tiles = vir_sym.shape[0]
    n_y = n_col // 4
    amp, block, meta = pack(amplitudes, integrals, pair_count, pair_sym, vir_sym, out_sym)

    def send(a, axis, hops, name):
        with jax.named_scope(name):
            return lax.ppermute(a, axis, hops)

    def across(a):
        return send(a, "col", [(c, (c + n_col // 2) % n_col) for c in range(n_col)], "across_x")

    def swap(a):
        return send(a, "col", [(c, c ^ 1) for c in range(n_col)], "swap_cores")

    def from_y(a, d):
        hops = [(c, c ^ (2 * d)) for c in range(n_col)]
        return send(a, "col", hops, f"from_y_{d}")

    def up(a, name):
        return send(a, "row", [(i, (i + 1) % n_row) for i in range(n_row)], "up_" + name)

    def down(a, name):
        return send(a, "row", [(i, (i - 1) % n_row) for i in range(n_row)], "down_" + name)

    def swap_slabs(a, step):
        return send(a, "slab", [(0, 1), (1, 0)], f"swap_slabs_{step}")

    half = TILE // 2
    other = swap_slabs(block, 0)
    below, above = up(block, "own_1"), down(block, "own_1")
    amp_two = join([join([amp], name="hold"), across(amp)], needed=[other], name="join_two", flops=3000000000)
    both = join([below, above], needed=[amp_two], name="join_own_1", flops=0)
    both_1, others_1 = both, swap_slabs(both, 1)
    below, above = up(join([(both, 0, TILE)], name="split"), "own_2"), down(join([(both, TILE, TILE)], name="split"), "own_2")
    amps = {0: amp_two, 1: from_y(amp_two, 1), 3: from_y(amp_two, 3)}
    both_2 = join([below, above], name="join_own_2", flops=5000000000)
    others_2 = swap_slabs(both_2, 2)
    below, above = up(join([(both_2, 0, TILE)], name="split"), "own_3"), down(join([(both_2, TILE, TILE)], name="split"), "own_3")
    amps[2] = from_y(join([amp_two], needed=[amps[1], amps[3]], name="hold"), 2)
    both_3 = join([below, above], needed=[others_1], name="join_own_3", flops=5000000000)
    low = up(join([(both_3, 0, half)], name="split"), "own_half")
    high = down(join([(both_3, TILE + half, half)], name="split"), "own_half")
    own_4 = join([low, high], name="join_own_4")
    other_4 = swap_slabs(own_4, 4)
    other_below = up(join([(others_2, 0, TILE)], name="split"), "other_3")
    other_above = down(join([(others_2, TILE, TILE)], name="split"), "other_3")

    amps = [join([amps[y]], needed=[both_3], name="hold") for y in range(n_y)]
    amps += [swap(a) for a in amps]
    first = {
        ((0, 0),): block,
        ((0, 1),): other,
        ((-1, 0), (1, 0)): both_1,
        ((-1, 1), (1, 1)): others_1,
        ((-2, 0), (2, 0)): both_2,
        ((-2, 1), (2, 1)): others_2,
        ((-3, 0), (3, 0)): both_3,
    }
    last = {((-4, 0),): own_4, ((-3, 1), (3, 1)): None, ((-4, 1),): other_4}
    acc, amp_all = early(rows, cols, k_tiles, list(first), meta, amps, list(first.values()))
    last[((-3, 1), (3, 1))] = join([other_below, other_above], needed=[acc], name="join_other_3", flops=4000000000)
    return late(rows, cols, k_tiles, list(last), meta, acc, amp_all, list(last.values()))


def solution(mesh):
    in_specs = (
        P("slab", "row", "col"),
        P(("row", "slab"), "col"),
        P(),
        P("slab", "row"),
        P(),
        P("col"),
    )
    out_specs = P("slab", "row", "col")
    return jax.shard_map(body, mesh=mesh, in_specs=in_specs, out_specs=out_specs, check_vma=False)
```
